512 devices in a mesh: ctx: 128 (over z, y, core), ch: 4 (over x).
Axes of the slice: x: 4, y: 4, z: 16, core: 2. Of those that a mesh axis runs over, the one named last changes fastest.
Arguments:
- query_proj: bfloat16 [16384, 4096], P('ctx', 'ch'), may hold values from -6 to 6
- key_proj: bfloat16 [16384, 4096], P('ctx', 'ch'), may hold values from -6 to 6
- value_proj: bfloat16 [16384, 4096], P('ctx', 'ch'), may hold values from -6 to 6
- decay_scale: float32 [16, 4096], P(None, 'ch'), may hold values from 0.25 to 512
- residues: float32 [16, 4096], P(None, 'ch'), may hold values from -1.5 to 1.5
- skip_gain: float32 [4096], P('ch'), may hold values from -4 to 4
- out_weight: bfloat16 [4096, 4096], P('ctx', 'ch'), may hold values from -0.09375 to 0.09375
Outputs:
- mixed: bfloat16 [16384, 4096], P('ctx', 'ch')
The draws below stay inside these ranges and needn't reach their ends.
All inputs are finite; a program needn't handle non-finite values.
Results may differ from the reference program's by a relative error of at most 0.019.
Values may be sent and summed in bfloat16 or wider, within the bound.
No kernel may reach another device: no remote copies, remote signals or barrier semaphores. Data moves between devices by JAX's collectives and lax.ppermute only.
A program may use at most 128 MiB of HBM per device.

```python
import math
import jax
import jax.numpy as jnp
from jax import lax

D = 4096
C = 4096
MODES = 16
SEQ = 16384


def steps_of(stream_key, dims, split, least, largest):
    def one(dim, blocks):
        steps = jax.random.uniform(jax.random.fold_in(jax.random.fold_in(stream_key, 6), dim), (blocks,), jnp.float32, least / len(split), largest / len(split))
        return jnp.repeat(jnp.exp(steps), dims[dim] // blocks).reshape((-1,) + (1,) * (len(dims) - dim - 1))

    factor_of = one(*split[0])
    for cut in split[1:]:
        factor_of = factor_of * one(*cut)
    return factor_of


def centred(stream_key, shape, spread, limit, split=(), kind=jnp.bfloat16):
    level = steps_of(stream_key, shape, split, -0.22, 0.18) if split else 1.0
    result = jax.random.normal(stream_key, shape, jnp.float32) * spread * level
    return jnp.minimum(jnp.maximum(result, -limit), limit).astype(kind)


def setup_inputs(seed: int = 0) -> dict:
    arg_keys = jax.random.split(jax.random.key(seed), 8)
    return {
        "query_proj": centred(arg_keys[0], (SEQ, C), 1.0, 6.0, ((0, 128), (1, 4))),
        "key_proj": centred(arg_keys[1], (SEQ, C), 1.0, 6.0, ((0, 128), (1, 4))),
        "value_proj": centred(arg_keys[2], (SEQ, C), 1.0, 6.0, ((0, 128), (1, 4))),
        "decay_scale": jnp.clip(jnp.exp(math.log(512.0) - 7.624619 * jax.random.uniform(arg_keys[3], (MODES, C), jnp.float32) ** steps_of(arg_keys[3], (MODES, C), ((1, 4),), -0.2, 0.2)), 0.25, 512.0),
        "residues": centred(arg_keys[4], (MODES, C), 0.25, 1.5, ((1, 4),), jnp.float32),
        "skip_gain": centred(arg_keys[5], (C,), 1.0, 4.0, ((0, 4),), jnp.float32),
        "out_weight": centred(arg_keys[6], (D, C), C ** -0.5, 0.09375, ((0, 128), (1, 4))),
    }


def reference(query_proj, key_proj, value_proj, decay_scale, residues, skip_gain, out_weight):
    product = (key_proj.astype(jnp.float32) * value_proj.astype(jnp.float32)).astype(jnp.bfloat16)
    seq_len = query_proj.shape[0]
    width = query_proj.shape[1]
    block = min(width, 256)
    count = width // block
    times = jnp.arange(seq_len).astype(jnp.float32)

    def conv_block(index):
        start = (index * block).astype(jnp.int32)
        piece = lax.dynamic_slice_in_dim(product, start, block, 1).astype(jnp.float32)
        rate = lax.dynamic_slice_in_dim(decay_scale, start, block, 1) / seq_len
        gain = lax.dynamic_slice_in_dim(residues, start, block, 1) * jnp.sqrt(2.0 * rate)

        def add_mode(mode, acc):
            return acc + gain[mode][None, :] * jnp.exp(-rate[mode][None, :] * times[:, None])
        filt = lax.fori_loop(0, MODES, add_mode, jnp.zeros((seq_len, block), jnp.float32))
        spectrum = jnp.fft.rfft(piece, n=2 * seq_len, axis=0) * jnp.fft.rfft(filt, n=2 * seq_len, axis=0)
        return jnp.fft.irfft(spectrum, n=2 * seq_len, axis=0)[:seq_len].astype(jnp.float32)
    blocks = lax.map(conv_block, jnp.arange(count).astype(jnp.int32))
    conv = jnp.moveaxis(blocks, 0, 1).reshape(seq_len, width).astype(jnp.bfloat16)
    gated = (query_proj.astype(jnp.float32) * (conv.astype(jnp.float32) + skip_gain[None, :] * product.astype(jnp.float32))).astype(jnp.bfloat16)
    mixed = lax.dot_general(gated, out_weight, (((1,), (1,)), ((), ())), preferred_element_type=jnp.float32)
    return mixed.astype(jnp.bfloat16)
```

```python
import jax
import jax.numpy as jnp
from jax import lax
from jax.experimental import pallas as pl
from jax.experimental.pallas import tpu as pltpu
from jax.sharding import Mesh
from jax.sharding import PartitionSpec as P

SEQ = 16384
F32 = jnp.float32
BF16 = jnp.bfloat16
VMEM = pl.BlockSpec(memory_space=pltpu.VMEM)
SMEM = pl.BlockSpec(memory_space=pltpu.SMEM)
PARAMS = pltpu.CompilerParams(vmem_limit_bytes=48 * 1024 * 1024)


def gain_of(scale, residues):
    return residues * jnp.sqrt(scale * (2.0 / SEQ))


def states_kernel(key_ref, value_ref, scale_ref, res_ref, out_ref, prod_ref):
    tokens, width = key_ref.shape
    modes = scale_ref.shape[0]
    product = key_ref[...].astype(F32) * value_ref[...].astype(F32)
    prod_ref[...] = product.astype(BF16).astype(F32)
    scale = scale_ref[...]
    decay = jnp.exp(scale * (-1.0 / SEQ))

    def step(t, state):
        return state * decay + prod_ref[pl.ds(t, 1), :]

    state = lax.fori_loop(0, tokens, step, jnp.zeros((modes, width), F32), unroll=8)
    state = state * gain_of(scale, res_ref[...])
    parts, _, lanes = out_ref.shape
    for part in range(parts):
        out_ref[part] = state[:, part * lanes : (part + 1) * lanes].astype(BF16)


def plane_kernel(states_ref, scale_ref, out_ref):
    parts = states_ref.shape[0]
    decay = jnp.exp(scale_ref[...] * (-1.0 / 128))
    total = states_ref[0].astype(F32)
    for part in range(1, parts):
        total = total * decay + states_ref[part].astype(F32)
    total = total.astype(BF16)
    for copy in range(out_ref.shape[0]):
        out_ref[copy] = total


def carry_kernel(plane_ref, totals_ref, states_ref, scale_ref, out_ref):
    plane = plane_ref[0]
    scale = scale_ref[...]
    decay = jnp.exp(scale * (-1.0 / 16))
    carry = jnp.zeros(scale.shape, F32)
    for other in range(totals_ref.shape[0]):
        carry = jnp.where(other < plane, carry * decay + totals_ref[other].astype(F32), carry)
    decay = jnp.exp(scale * (-1.0 / 128))
    for part in range(states_ref.shape[0]):
        out_ref[part] = carry.astype(BF16)
        carry = carry * decay + states_ref[part].astype(F32)


def gated_kernel(
    query_ref, key_ref, value_ref, scale_ref, res_ref, skip_ref, carry_ref, out_ref, prod_ref, conv_ref
):
    tokens, width = key_ref.shape
    parts, _, lanes = carry_ref.shape
    product = key_ref[...].astype(F32) * value_ref[...].astype(F32)
    prod_ref[...] = product.astype(BF16).astype(F32)
    scale = scale_ref[...]
    decay = jnp.exp(scale * (-1.0 / SEQ))
    gain = gain_of(scale, res_ref[...])
    start = jnp.concatenate([carry_ref[part].astype(F32) for part in range(parts)], axis=1)

    def step(t, state):
        state = state * decay + gain * prod_ref[pl.ds(t, 1), :]
        conv_ref[pl.ds(t, 1), :] = jnp.sum(state, axis=0, keepdims=True)
        return state

    lax.fori_loop(0, tokens, step, start, unroll=8)
    out_ref[...] = (
        query_ref[...].astype(F32) * (conv_ref[...] + skip_ref[...] * prod_ref[...])
    ).astype(BF16)


def project_kernel(gated_ref, weight_ref, out_ref):
    blocks = gated_ref.shape[0]
    pieces, _, lanes = out_ref.shape
    quarters = pieces // blocks
    for quarter in range(quarters):
        rows = weight_ref[quarter * lanes : (quarter + 1) * lanes, :]
        for block in range(blocks):
            out_ref[block * quarters + quarter] = lax.dot_general(
                gated_ref[block], rows, (((1,), (1,)), ((), ())), preferred_element_type=F32
            ).astype(BF16)


def sum_kernel(pieces_ref, out_ref):
    quarters = 4
    for row in range(quarters):
        total = pieces_ref[row * 4].astype(F32)
        for owner in range(1, 4):
            total = total + pieces_ref[row * 4 + owner].astype(F32)
        total = total.astype(BF16)
        for plane in range(4):
            start = plane * 256 + row * 64
            out_ref[:, start : start + 64] = total[:, plane * 64 : plane * 64 + 64]


def call(kernel, shape, inputs, specs=None, scratch=(), dtype=BF16):
    return pl.pallas_call(
        kernel,
        out_shape=jax.ShapeDtypeStruct(shape, dtype),
        in_specs=specs or [VMEM] * len(inputs),
        out_specs=VMEM,
        scratch_shapes=list(scratch),
        compiler_params=PARAMS,
    )(*inputs)


def exchange(pieces, axes):
    return lax.all_to_all(pieces, axes, split_axis=0, concat_axis=0, tiled=True)


def body(query, key, value, scale, residues, skip, out_weight):
    tokens, width = query.shape
    modes = scale.shape[0]
    near = ("y", "core")
    lanes = width // 8
    weight = lax.all_gather(out_weight, ("z", "core"), axis=0, tiled=True)
    work = pltpu.VMEM((tokens, width), F32)
    states = call(states_kernel, (8, modes, lanes), (key, value, scale, residues), scratch=[work])
    states = exchange(states, near)
    own = lax.axis_index(near)
    own_scale = lax.dynamic_slice_in_dim(scale, own * lanes, lanes, 1)
    totals = call(plane_kernel, (16, modes, lanes), (states, own_scale))
    totals = exchange(totals, "z")
    plane = lax.axis_index("z").astype(jnp.int32).reshape(1)
    carry = call(
        carry_kernel,
        (8, modes, lanes),
        (plane, totals, states, own_scale),
        specs=[SMEM, VMEM, VMEM, VMEM],
    )
    carry = exchange(carry, near)
    gated = call(
        gated_kernel,
        (tokens, width),
        (query, key, value, scale, residues, skip.reshape(1, width), carry),
        scratch=[work, work],
    )
    gated = exchange(jnp.broadcast_to(gated[None], (4, tokens, width)), "y")
    terms = call(project_kernel, (16, tokens, 256), (gated, weight))
    terms = exchange(terms, ("y", "x"))
    return call(sum_kernel, (tokens, width), (terms,))


def solution(mesh):
    fine = Mesh(mesh.devices.reshape(16, 4, 2, 4), ("z", "y", "core", "x"))
    both = P(("z", "y", "core"), "x")
    placed = (both, both, both, P(None, "x"), P(None, "x"), P("x"), both)
    return jax.shard_map(body, mesh=fine, in_specs=placed, out_specs=both, check_vma=False)
```

```python
import jax
import jax.numpy as jnp
from jax import lax
from jax.experimental import pallas as pl
from jax.experimental.pallas import tpu as pltpu
from jax.sharding import Mesh
from jax.sharding import PartitionSpec as P

SEQ = 16384
F32 = jnp.float32
BF16 = jnp.bfloat16
VMEM = pl.BlockSpec(memory_space=pltpu.VMEM)
HBM = pl.BlockSpec(memory_space=pltpu.HBM)
SMEM = pl.BlockSpec(memory_space=pltpu.SMEM)
NEAR = ("y", "core")
PLANES = ("zp", "zq")


def gain_of(scale, residues):
    return residues * jnp.sqrt(scale * (2.0 / SEQ))


def product_kernel(
    key_hbm, value_hbm, query_hbm, weight_hbm, out_ref, copy_hbm, key_ref, value_ref, query_ref, sems
):
    loads = [
        pltpu.make_async_copy(src, dst, sems.at[i])
        for i, (src, dst) in enumerate(
            ((key_hbm, key_ref), (value_hbm, value_ref), (query_hbm, query_ref), (weight_hbm, copy_hbm))
        )
    ]
    for load in loads:
        load.start()
    for load in loads[:3]:
        load.wait()
    tokens = key_ref.shape[0]
    parts, _, lanes = out_ref.shape
    for part in range(parts):
        cols = slice(part * lanes, (part + 1) * lanes)
        product = key_ref[:, cols].astype(F32) * value_ref[:, cols].astype(F32)
        out_ref[part, :tokens] = product.astype(BF16)
        out_ref[part, tokens:] = query_ref[:, cols]
    loads[3].wait()


def states_kernel(slices_ref, scale_ref, res_ref, totals_ref, states_ref, prod_ref):
    parts, tokens, lanes = prod_ref.shape
    modes = scale_ref.shape[0]
    prod_ref[...] = slices_ref[:, :tokens].astype(F32)
    scale = scale_ref[...]
    decay = jnp.exp(scale * (-1.0 / SEQ))
    gain = gain_of(scale, res_ref[...])

    def step(t, states):
        return tuple(
            state * decay + prod_ref[part, pl.ds(t, 1), :] for part, state in enumerate(states)
        )

    zero = jnp.zeros((modes, lanes), F32)
    states = lax.fori_loop(0, tokens, step, (zero,) * parts, unroll=8)
    decay = jnp.exp(scale * (-1.0 / 128))
    total = zero
    for part in range(parts):
        state = states[part] * gain
        states_ref[part] = state
        total = total * decay + state
    total = total.astype(BF16)
    for copy in range(totals_ref.shape[0]):
        totals_ref[copy] = total


def local_kernel(
    slices_ref, states_ref, scale_ref, res_ref, skip_ref, base_ref, powers_ref, prod_ref
):
    parts, tokens, lanes = prod_ref.shape
    modes = scale_ref.shape[0]
    prod_ref[...] = slices_ref[:, :tokens].astype(F32)
    scale = scale_ref[...]
    decay = jnp.exp(scale * (-1.0 / SEQ))
    gain = gain_of(scale, res_ref[...])
    leap = jnp.exp(scale * (-1.0 / 128))
    starts = [jnp.zeros((modes, lanes), F32)]
    for part in range(parts - 1):
        starts.append(starts[-1] * leap + states_ref[part])

    def step(t, states):
        fresh = []
        for part, state in enumerate(states):
            state = state * decay + gain * prod_ref[part, pl.ds(t, 1), :]
            base_ref[part, pl.ds(t, 1), :] = jnp.sum(state, axis=0, keepdims=True)
            fresh.append(state)
        return tuple(fresh)

    lax.fori_loop(0, tokens, step, tuple(starts), unroll=4)
    skip = skip_ref[...]
    for part in range(parts):
        base_ref[part] = base_ref[part] + skip * prod_ref[part]
    ages = (lax.broadcasted_iota(jnp.int32, (tokens, lanes), 0) + 1).astype(F32) * (-1.0 / SEQ)
    for mode in range(modes):
        powers_ref[mode] = jnp.exp(ages * scale[mode : mode + 1, :])


def gated_kernel(plane_ref, totals_ref, slices_ref, base_ref, powers_ref, scale_ref, out_ref):
    plane = plane_ref[0]
    parts, tokens, lanes = base_ref.shape
    modes = scale_ref.shape[0]
    scale = scale_ref[...]
    leap = jnp.exp(scale * (-1.0 / 16))
    carry = jnp.zeros(scale.shape, F32)
    for other in range(totals_ref.shape[0]):
        carry = jnp.where(other < plane, carry * leap + totals_ref[other].astype(F32), carry)
    leap = jnp.exp(scale * (-1.0 / 128))
    for part in range(parts):
        conv = base_ref[part]
        for mode in range(modes):
            conv = conv + powers_ref[mode] * carry[mode : mode + 1, :]
        gated = (slices_ref[part, tokens:].astype(F32) * conv).astype(BF16)
        for row in range(4):
            out_ref[2 * row + part % 2, part // 2] = gated
        carry = carry * leap


def project_kernel(gated_ref, weight_hbm, out_ref, rows_ref, weight_ref, sems):
    parts, blocks, tokens, lanes = gated_ref.shape
    loads = [
        pltpu.make_async_copy(
            weight_hbm.at[256 * quarter : 256 * quarter + 256], weight_ref.at[quarter], sems.at[quarter]
        )
        for quarter in range(4)
    ]
    for load in loads:
        load.start()
    for block in range(blocks):
        for part in range(parts):
            rows_ref[block * tokens : (block + 1) * tokens, part * lanes : (part + 1) * lanes] = (
                gated_ref[part, block]
            )
    order = [4 * far + 2 * core + near for far in range(2) for near in range(2) for core in range(2)]
    for quarter in range(4):
        loads[quarter].wait()
        weight = jnp.concatenate([weight_ref[quarter, 32 * i : 32 * i + 32, :] for i in order], axis=0)
        terms = lax.dot_general(
            rows_ref[...], weight, (((1,), (1,)), ((), ())), preferred_element_type=F32
        ).astype(BF16)
        for block in range(blocks):
            out_ref[block * 4 + quarter] = terms[block * tokens : (block + 1) * tokens]


def sum_kernel(pieces_ref, out_ref):
    for row in range(4):
        total = pieces_ref[row * 4].astype(F32)
        for owner in range(1, 4):
            total = total + pieces_ref[row * 4 + owner].astype(F32)
        total = total.astype(BF16)
        for plane in range(4):
            start = plane * 256 + row * 64
            out_ref[:, start : start + 64] = total[:, plane * 64 : plane * 64 + 64]


def call(kernel, outs, inputs, specs=None, scratch=(), cost=None, out_spec=None, limit=48):
    single = not isinstance(outs, list)
    return pl.pallas_call(
        kernel,
        out_shape=outs,
        in_specs=specs or [VMEM] * len(inputs),
        out_specs=out_spec or (VMEM if single else [VMEM] * len(outs)),
        scratch_shapes=list(scratch),
        compiler_params=pltpu.CompilerParams(vmem_limit_bytes=int(limit * 1024 * 1024)),
        cost_estimate=cost,
    )(*inputs)


def arr(*shape, dtype=BF16):
    return jax.ShapeDtypeStruct(shape, dtype)


def exchange(pieces, axes):
    return lax.all_to_all(pieces, axes, split_axis=0, concat_axis=0, tiled=True)


def body(query, key, value, scale, residues, skip, out_weight):
    tokens, width = query.shape
    modes = scale.shape[0]
    lanes = width // 8
    other = lax.ppermute(out_weight, "zq", [(0, 1), (1, 0)])
    z = lax.axis_index(PLANES).astype(jnp.int32)
    load = pltpu.VMEM((tokens, width), BF16)
    slices, same = call(
        product_kernel,
        [arr(8, 2 * tokens, lanes), arr(32, width)],
        (key, value, query, out_weight),
        specs=[HBM] * 4,
        scratch=[load, load, load, pltpu.SemaphoreType.DMA((4,))],
        out_spec=[VMEM, HBM],
        limit=62,
        cost=pl.CostEstimate(flops=2_000_000, bytes_accessed=4_000_000, transcendentals=0),
    )
    pair = jnp.where(
        z % 2 == 0, jnp.concatenate([same, other], axis=0), jnp.concatenate([other, same], axis=0)
    )
    weight = lax.all_gather(pair, ("zp", "core"), axis=0, tiled=True)
    slices = exchange(slices, NEAR)
    own = lax.axis_index(NEAR) * lanes
    scale, residues, skip = (
        lax.dynamic_slice_in_dim(a, own, lanes, 1) for a in (scale, residues, skip.reshape(1, width))
    )
    work = pltpu.VMEM((8, tokens, lanes), F32)
    totals, states = call(
        states_kernel,
        [arr(16, modes, lanes), arr(8, modes, lanes, dtype=F32)],
        (slices, scale, residues),
        scratch=[work],
    )
    totals = exchange(totals, PLANES)
    base, powers = call(
        local_kernel,
        [arr(8, tokens, lanes, dtype=F32), arr(modes, tokens, lanes, dtype=F32)],
        (slices, states, scale, residues, skip),
        scratch=[work],
        cost=pl.CostEstimate(flops=20_000_000, bytes_accessed=2_000_000, transcendentals=300_000),
    )
    gated = call(
        gated_kernel,
        arr(8, 4, tokens, lanes),
        (z.reshape(1), totals, slices, base, powers, scale),
        specs=[SMEM] + [VMEM] * 5,
    )
    gated = exchange(gated, NEAR)
    terms = call(
        project_kernel,
        arr(16, tokens, 256),
        (gated, weight),
        specs=[VMEM, HBM],
        scratch=[
            pltpu.VMEM((4 * tokens, width), BF16),
            pltpu.VMEM((4, 256, width), BF16),
            pltpu.SemaphoreType.DMA((4,)),
        ],
        limit=50.5,
    )
    terms = exchange(terms, ("y", "x"))
    return call(sum_kernel, arr(tokens, width), (terms,))


def solution(mesh):
    fine = Mesh(mesh.devices.reshape(8, 2, 4, 2, 4), ("zp", "zq", "y", "core", "x"))
    both = P(("zp", "zq", "y", "core"), "x")
    placed = (both, both, both, P(None, "x"), P(None, "x"), P("x"), both)
    return jax.shard_map(body, mesh=fine, in_specs=placed, out_specs=both, check_vma=False)
```

```python
import jax
import jax.numpy as jnp
from jax import lax
from jax.experimental import pallas as pl
from jax.experimental.pallas import tpu as pltpu
from jax.sharding import Mesh
from jax.sharding import PartitionSpec as P

SEQ = 16384
F32 = jnp.float32
BF16 = jnp.bfloat16
VMEM = pl.BlockSpec(memory_space=pltpu.VMEM)
HBM = pl.BlockSpec(memory_space=pltpu.HBM)
SMEM = pl.BlockSpec(memory_space=pltpu.SMEM)
NEAR = ("y", "core")
PLANES = ("zp", "zq")


def gain_of(scale, residues):
    return residues * jnp.sqrt(scale * (2.0 / SEQ))


def product_kernel(
    key_hbm, value_hbm, query_hbm, weight_hbm, out_ref, copy_ref, key_ref, value_ref, query_ref, weight_ref, sems
):
    loads = [
        pltpu.make_async_copy(src, dst, sems.at[i])
        for i, (src, dst) in enumerate(
            ((key_hbm, key_ref), (value_hbm, value_ref), (query_hbm, query_ref), (weight_hbm, weight_ref))
        )
    ]
    for load in loads:
        load.start()
    for load in loads:
        load.wait()
    tokens = key_ref.shape[0]
    parts, _, lanes = out_ref.shape
    for part in range(parts):
        cols = slice(part * lanes, (part + 1) * lanes)
        product = key_ref[:, cols].astype(F32) * value_ref[:, cols].astype(F32)
        out_ref[part, :tokens] = product.astype(BF16)
        out_ref[part, tokens:] = query_ref[:, cols]
    copy_ref[...] = weight_ref[...]


def states_kernel(slices_ref, scale_ref, res_ref, totals_ref, states_ref, prod_ref):
    parts, tokens, lanes = prod_ref.shape
    modes = scale_ref.shape[0]
    prod_ref[...] = slices_ref[:, :tokens].astype(F32)
    scale = scale_ref[...]
    decay = jnp.exp(scale * (-1.0 / SEQ))
    gain = gain_of(scale, res_ref[...])

    def step(t, states):
        return tuple(
            state * decay + prod_ref[part, pl.ds(t, 1), :] for part, state in enumerate(states)
        )

    zero = jnp.zeros((modes, lanes), F32)
    states = lax.fori_loop(0, tokens, step, (zero,) * parts, unroll=8)
    decay = jnp.exp(scale * (-1.0 / 128))
    total = zero
    for part in range(parts):
        state = states[part] * gain
        states_ref[part] = state
        total = total * decay + state
    total = total.astype(BF16)
    for copy in range(totals_ref.shape[0]):
        totals_ref[copy] = total


def local_kernel(
    slices_ref, states_ref, scale_ref, res_ref, skip_ref, base_ref, powers_ref, prod_ref
):
    parts, tokens, lanes = prod_ref.shape
    modes = scale_ref.shape[0]
    prod_ref[...] = slices_ref[:, :tokens].astype(F32)
    scale = scale_ref[...]
    decay = jnp.exp(scale * (-1.0 / SEQ))
    gain = gain_of(scale, res_ref[...])
    leap = jnp.exp(scale * (-1.0 / 128))
    starts = [jnp.zeros((modes, lanes), F32)]
    for part in range(parts - 1):
        starts.append(starts[-1] * leap + states_ref[part])

    def step(t, states):
        fresh = []
        for part, state in enumerate(states):
            state = state * decay + gain * prod_ref[part, pl.ds(t, 1), :]
            base_ref[part, pl.ds(t, 1), :] = jnp.sum(state, axis=0, keepdims=True)
            fresh.append(state)
        return tuple(fresh)

    lax.fori_loop(0, tokens, step, tuple(starts), unroll=4)
    skip = skip_ref[...]
    for part in range(parts):
        base_ref[part] = base_ref[part] + skip * prod_ref[part]
    ages = (lax.broadcasted_iota(jnp.int32, (tokens, lanes), 0) + 1).astype(F32) * (-1.0 / SEQ)
    for mode in range(modes):
        powers_ref[mode] = jnp.exp(ages * scale[mode : mode + 1, :])


def gated_kernel(plane_ref, totals_ref, slices_ref, base_ref, powers_ref, scale_ref, out_ref):
    plane = plane_ref[0]
    parts, tokens, lanes = base_ref.shape
    modes = scale_ref.shape[0]
    scale = scale_ref[...]
    leap = jnp.exp(scale * (-1.0 / 16))
    carry = jnp.zeros(scale.shape, F32)
    for other in range(totals_ref.shape[0]):
        carry = jnp.where(other < plane, carry * leap + totals_ref[other].astype(F32), carry)
    leap = jnp.exp(scale * (-1.0 / 128))
    for part in range(parts):
        conv = base_ref[part]
        for mode in range(modes):
            conv = conv + powers_ref[mode] * carry[mode : mode + 1, :]
        gated = (slices_ref[part, tokens:].astype(F32) * conv).astype(BF16)
        for row in range(4):
            out_ref[2 * row + part % 2, part // 2] = gated
        carry = carry * leap


def project_kernel(gated_ref, weight_hbm, out_ref, rows_ref, weight_ref, sems):
    parts, blocks, tokens, lanes = gated_ref.shape
    loads = [
        pltpu.make_async_copy(
            weight_hbm.at[256 * quarter : 256 * quarter + 256], weight_ref.at[quarter], sems.at[quarter]
        )
        for quarter in range(4)
    ]
    for load in loads:
        load.start()
    for block in range(blocks):
        for part in range(parts):
            rows_ref[block * tokens : (block + 1) * tokens, part * lanes : (part + 1) * lanes] = (
                gated_ref[part, block]
            )
    order = [4 * far + 2 * core + near for far in range(2) for near in range(2) for core in range(2)]
    for half in range(2):
        quarters = (2 * half, 2 * half + 1)
        for quarter in quarters:
            loads[quarter].wait()
        weight = jnp.concatenate(
            [weight_ref[quarter, 32 * i : 32 * i + 32, :] for quarter in quarters for i in order], axis=0
        )
        terms = lax.dot_general(
            rows_ref[...], weight, (((1,), (1,)), ((), ())), preferred_element_type=F32
        ).astype(BF16)
        for i, quarter in enumerate(quarters):
            for block in range(blocks):
                out_ref[block * 4 + quarter] = terms[
                    block * tokens : (block + 1) * tokens, 256 * i : 256 * i + 256
                ]


def sum_kernel(pieces_ref, out_ref):
    for row in range(4):
        total = pieces_ref[row * 4].astype(F32)
        for owner in range(1, 4):
            total = total + pieces_ref[row * 4 + owner].astype(F32)
        total = total.astype(BF16)
        for plane in range(4):
            start = plane * 256 + row * 64
            out_ref[:, start : start + 64] = total[:, plane * 64 : plane * 64 + 64]


def call(kernel, outs, inputs, specs=None, scratch=(), cost=None, out_spec=None, limit=48):
    single = not isinstance(outs, list)
    return pl.pallas_call(
        kernel,
        out_shape=outs,
        in_specs=specs or [VMEM] * len(inputs),
        out_specs=out_spec or (VMEM if single else [VMEM] * len(outs)),
        scratch_shapes=list(scratch),
        compiler_params=pltpu.CompilerParams(vmem_limit_bytes=int(limit * 1024 * 1024)),
        cost_estimate=cost,
    )(*inputs)


def arr(*shape, dtype=BF16):
    return jax.ShapeDtypeStruct(shape, dtype)


def exchange(pieces, axes):
    return lax.all_to_all(pieces, axes, split_axis=0, concat_axis=0, tiled=True)


def body(query, key, value, scale, residues, skip, out_weight):
    tokens, width = query.shape
    modes = scale.shape[0]
    lanes = width // 8
    z = lax.axis_index(PLANES).astype(jnp.int32)
    load = pltpu.VMEM((tokens, width), BF16)
    slices, same = call(
        product_kernel,
        [arr(8, 2 * tokens, lanes), arr(32, width)],
        (key, value, query, out_weight),
        specs=[HBM] * 4,
        scratch=[load, load, load, pltpu.VMEM((32, width), BF16), pltpu.SemaphoreType.DMA((4,))],
        limit=62,
        cost=pl.CostEstimate(flops=2_000_000, bytes_accessed=4_000_000, transcendentals=0),
    )
    other = lax.ppermute(out_weight, "zq", [(0, 1), (1, 0)])
    pair = jnp.where(
        z % 2 == 0,
        jnp.concatenate([same, other], axis=0),
        jnp.concatenate([other, same], axis=0),
    )
    weight = lax.all_gather(pair, ("zp", "core"), axis=0, tiled=True)
    slices = exchange(slices, NEAR)
    own = lax.axis_index(NEAR) * lanes
    scale, residues, skip = (
        lax.dynamic_slice_in_dim(a, own, lanes, 1) for a in (scale, residues, skip.reshape(1, width))
    )
    work = pltpu.VMEM((8, tokens, lanes), F32)
    totals, states = call(
        states_kernel,
        [arr(16, modes, lanes), arr(8, modes, lanes, dtype=F32)],
        (slices, scale, residues),
        scratch=[work],
        cost=pl.CostEstimate(flops=20_000_000, bytes_accessed=2_000_000, transcendentals=0),
    )
    totals = exchange(totals, PLANES)
    base, powers = call(
        local_kernel,
        [arr(8, tokens, lanes, dtype=F32), arr(modes, tokens, lanes, dtype=F32)],
        (slices, states, scale, residues, skip),
        scratch=[work],
        cost=pl.CostEstimate(flops=20_000_000, bytes_accessed=2_000_000, transcendentals=300_000),
    )
    gated = call(
        gated_kernel,
        arr(8, 4, tokens, lanes),
        (z.reshape(1), totals, slices, base, powers, scale),
        specs=[SMEM] + [VMEM] * 5,
    )
    gated = exchange(gated, NEAR)
    terms = call(
        project_kernel,
        arr(16, tokens, 256),
        (gated, weight),
        specs=[VMEM, HBM],
        scratch=[
            pltpu.VMEM((4 * tokens, width), BF16),
            pltpu.VMEM((4, 256, width), BF16),
            pltpu.SemaphoreType.DMA((4,)),
        ],
        limit=50.5,
    )
    terms = exchange(terms, ("y", "x"))
    return call(sum_kernel, arr(tokens, width), (terms,))


def solution(mesh):
    fine = Mesh(mesh.devices.reshape(8, 2, 4, 2, 4), ("zp", "zq", "y", "core", "x"))
    both = P(("zp", "zq", "y", "core"), "x")
    placed = (both, both, both, P(None, "x"), P(None, "x"), P("x"), both)
    return jax.shard_map(body, mesh=fine, in_specs=placed, out_specs=both, check_vma=False)
```

```python
import jax
import jax.numpy as jnp
from jax import lax
from jax.experimental import pallas as pl
from jax.experimental.pallas import tpu as pltpu
from jax.sharding import Mesh
from jax.sharding import PartitionSpec as P

SEQ = 16384
F32 = jnp.float32
BF16 = jnp.bfloat16
VMEM = pl.BlockSpec(memory_space=pltpu.VMEM)
HBM = pl.BlockSpec(memory_space=pltpu.HBM)
SMEM = pl.BlockSpec(memory_space=pltpu.SMEM)
NEAR = ("y", "core")
PLANES = ("zp", "zq")


def gain_of(scale, residues):
    return residues * jnp.sqrt(scale * (2.0 / SEQ))


def product_kernel(
    near_ref,
    key_hbm,
    value_hbm,
    query_hbm,
    weight_hbm,
    out_ref,
    pair_hbm,
    key_ref,
    value_ref,
    query_ref,
    weight_ref,
    sems,
):
    loads = [
        pltpu.make_async_copy(src, dst, sems.at[i])
        for i, (src, dst) in enumerate(
            ((key_hbm, key_ref), (value_hbm, value_ref), (query_hbm, query_ref), (weight_hbm, weight_ref))
        )
    ]
    for load in loads:
        load.start()
    for load in loads:
        load.wait()
    rows = weight_hbm.shape[0]
    half = pair_hbm.at[pl.ds(pl.multiple_of(near_ref[0] * rows, rows), rows)]
    store = pltpu.make_async_copy(weight_ref, half, sems.at[4])
    store.start()
    tokens = key_ref.shape[0]
    parts, _, lanes = out_ref.shape
    for part in range(parts):
        cols = slice(part * lanes, (part + 1) * lanes)
        product = key_ref[:, cols].astype(F32) * value_ref[:, cols].astype(F32)
        out_ref[part, :tokens] = product.astype(BF16)
        out_ref[part, tokens:] = query_ref[:, cols]
    store.wait()


def states_kernel(slices_ref, scale_ref, res_ref, totals_ref, states_ref, prod_ref):
    parts, tokens, lanes = prod_ref.shape
    modes = scale_ref.shape[0]
    prod_ref[...] = slices_ref[:, :tokens].astype(F32)
    scale = scale_ref[...]
    decay = jnp.exp(scale * (-1.0 / SEQ))
    gain = gain_of(scale, res_ref[...])

    def step(t, states):
        return tuple(
            state * decay + prod_ref[part, pl.ds(t, 1), :] for part, state in enumerate(states)
        )

    zero = jnp.zeros((modes, lanes), F32)
    states = lax.fori_loop(0, tokens, step, (zero,) * parts, unroll=8)
    decay = jnp.exp(scale * (-1.0 / 128))
    total = zero
    for part in range(parts):
        state = states[part] * gain
        states_ref[part] = state
        total = total * decay + state
    total = total.astype(BF16)
    for copy in range(totals_ref.shape[0]):
        totals_ref[copy] = total


def local_kernel(
    slices_ref, states_ref, scale_ref, res_ref, skip_ref, base_ref, powers_ref, prod_ref
):
    parts, tokens, lanes = prod_ref.shape
    modes = scale_ref.shape[0]
    prod_ref[...] = slices_ref[:, :tokens].astype(F32)
    scale = scale_ref[...]
    decay = jnp.exp(scale * (-1.0 / SEQ))
    gain = gain_of(scale, res_ref[...])
    leap = jnp.exp(scale * (-1.0 / 128))
    starts = [jnp.zeros((modes, lanes), F32)]
    for part in range(parts - 1):
        starts.append(starts[-1] * leap + states_ref[part])

    def step(t, states):
        fresh = []
        for part, state in enumerate(states):
            state = state * decay + gain * prod_ref[part, pl.ds(t, 1), :]
            base_ref[part, pl.ds(t, 1), :] = jnp.sum(state, axis=0, keepdims=True)
            fresh.append(state)
        return tuple(fresh)

    lax.fori_loop(0, tokens, step, tuple(starts), unroll=4)
    skip = skip_ref[...]
    for part in range(parts):
        base_ref[part] = base_ref[part] + skip * prod_ref[part]
    ages = (lax.broadcasted_iota(jnp.int32, (tokens, lanes), 0) + 1).astype(F32) * (-1.0 / SEQ)
    for mode in range(modes):
        powers_ref[mode] = jnp.exp(ages * scale[mode : mode + 1, :])


def gated_kernel(plane_ref, totals_ref, slices_ref, base_ref, powers_ref, scale_ref, out_ref):
    plane = plane_ref[0]
    parts, tokens, lanes = base_ref.shape
    modes = scale_ref.shape[0]
    scale = scale_ref[...]
    leap = jnp.exp(scale * (-1.0 / 16))
    carry = jnp.zeros(scale.shape, F32)
    for other in range(totals_ref.shape[0]):
        carry = jnp.where(other < plane, carry * leap + totals_ref[other].astype(F32), carry)
    leap = jnp.exp(scale * (-1.0 / 128))
    for part in range(parts):
        conv = base_ref[part]
        for mode in range(modes):
            conv = conv + powers_ref[mode] * carry[mode : mode + 1, :]
        gated = (slices_ref[part, tokens:].astype(F32) * conv).astype(BF16)
        for row in range(4):
            out_ref[2 * row + part % 2, part // 2] = gated
        carry = carry * leap


def project_kernel(gated_ref, weight_hbm, out_ref, rows_ref, weight_ref, sems):
    parts, blocks, tokens, lanes = gated_ref.shape
    loads = [
        pltpu.make_async_copy(
            weight_hbm.at[256 * quarter : 256 * quarter + 256], weight_ref.at[quarter], sems.at[quarter]
        )
        for quarter in range(4)
    ]
    for load in loads:
        load.start()
    for block in range(blocks):
        for part in range(parts):
            rows_ref[block * tokens : (block + 1) * tokens, part * lanes : (part + 1) * lanes] = (
                gated_ref[part, block]
            )
    order = [4 * far + 2 * core + near for far in range(2) for near in range(2) for core in range(2)]
    for half in range(2):
        quarters = (2 * half, 2 * half + 1)
        for quarter in quarters:
            loads[quarter].wait()
        weight = jnp.concatenate(
            [weight_ref[quarter, 32 * i : 32 * i + 32, :] for quarter in quarters for i in order], axis=0
        )
        terms = lax.dot_general(
            rows_ref[...], weight, (((1,), (1,)), ((), ())), preferred_element_type=F32
        ).astype(BF16)
        for i, quarter in enumerate(quarters):
            for block in range(blocks):
                out_ref[block * 4 + quarter] = terms[
                    block * tokens : (block + 1) * tokens, 256 * i : 256 * i + 256
                ]


def sum_kernel(pieces_ref, out_ref):
    for row in range(4):
        total = pieces_ref[row * 4].astype(F32)
        for owner in range(1, 4):
            total = total + pieces_ref[row * 4 + owner].astype(F32)
        total = total.astype(BF16)
        for plane in range(4):
            start = plane * 256 + row * 64
            out_ref[:, start : start + 64] = total[:, plane * 64 : plane * 64 + 64]


def call(kernel, outs, inputs, specs=None, scratch=(), cost=None, out_spec=None, limit=48):
    single = not isinstance(outs, list)
    return pl.pallas_call(
        kernel,
        out_shape=outs,
        in_specs=specs or [VMEM] * len(inputs),
        out_specs=out_spec or (VMEM if single else [VMEM] * len(outs)),
        scratch_shapes=list(scratch),
        compiler_params=pltpu.CompilerParams(vmem_limit_bytes=int(limit * 1024 * 1024)),
        cost_estimate=cost,
    )(*inputs)


def arr(*shape, dtype=BF16):
    return jax.ShapeDtypeStruct(shape, dtype)


def exchange(pieces, axes):
    return lax.all_to_all(pieces, axes, split_axis=0, concat_axis=0, tiled=True)


def body(query, key, value, scale, residues, skip, out_weight):
    tokens, width = query.shape
    modes = scale.shape[0]
    lanes = width // 8
    z = lax.axis_index(PLANES).astype(jnp.int32)
    load = pltpu.VMEM((tokens, width), BF16)
    near = z.reshape(1) % 2
    slices, half = call(
        product_kernel,
        [arr(8, 2 * tokens, lanes), arr(64, width)],
        (near, key, value, query, out_weight),
        specs=[SMEM] + [HBM] * 4,
        scratch=[load, load, load, pltpu.VMEM((32, width), BF16), pltpu.SemaphoreType.DMA((5,))],
        limit=62,
        cost=pl.CostEstimate(flops=2_000_000, bytes_accessed=4_000_000, transcendentals=0),
    )
    other = lax.ppermute(out_weight, "zq", [(0, 1), (1, 0)])
    pair = lax.dynamic_update_slice_in_dim(half, other, (1 - z % 2) * out_weight.shape[0], 0)
    weight = lax.all_gather(pair, ("zp", "core"), axis=0, tiled=True)
    slices = exchange(slices, NEAR)
    own = lax.axis_index(NEAR) * lanes
    scale, residues, skip = (
        lax.dynamic_slice_in_dim(a, own, lanes, 1) for a in (scale, residues, skip.reshape(1, width))
    )
    work = pltpu.VMEM((8, tokens, lanes), F32)
    totals, states = call(
        states_kernel,
        [arr(16, modes, lanes), arr(8, modes, lanes, dtype=F32)],
        (slices, scale, residues),
        scratch=[work],
        cost=pl.CostEstimate(flops=20_000_000, bytes_accessed=2_000_000, transcendentals=0),
    )
    totals = exchange(totals, PLANES)
    base, powers = call(
        local_kernel,
        [arr(8, tokens, lanes, dtype=F32), arr(modes, tokens, lanes, dtype=F32)],
        (slices, states, scale, residues, skip),
        scratch=[work],
        cost=pl.CostEstimate(flops=20_000_000, bytes_accessed=2_000_000, transcendentals=300_000),
    )
    gated = call(
        gated_kernel,
        arr(8, 4, tokens, lanes),
        (z.reshape(1), totals, slices, base, powers, scale),
        specs=[SMEM] + [VMEM] * 5,
    )
    gated = exchange(gated, NEAR)
    terms = call(
        project_kernel,
        arr(16, tokens, 256),
        (gated, weight),
        specs=[VMEM, HBM],
        scratch=[
            pltpu.VMEM((4 * tokens, width), BF16),
            pltpu.VMEM((4, 256, width), BF16),
            pltpu.SemaphoreType.DMA((4,)),
        ],
        limit=50.5,
    )
    terms = exchange(terms, ("y", "x"))
    return call(sum_kernel, arr(tokens, width), (terms,))


def solution(mesh):
    fine = Mesh(mesh.devices.reshape(8, 2, 4, 2, 4), ("zp", "zq", "y", "core", "x"))
    both = P(("zp", "zq", "y", "core"), "x")
    placed = (both, both, both, P(None, "x"), P(None, "x"), P("x"), both)
    return jax.shard_map(body, mesh=fine, in_specs=placed, out_specs=both, check_vma=False)
```

```python
import jax
import jax.numpy as jnp
from jax import lax
from jax.experimental import pallas as pl
from jax.experimental.pallas import tpu as pltpu
from jax.sharding import Mesh
from jax.sharding import PartitionSpec as P

SEQ = 16384
F32 = jnp.float32
BF16 = jnp.bfloat16
VMEM = pl.BlockSpec(memory_space=pltpu.VMEM)
HBM = pl.BlockSpec(memory_space=pltpu.HBM)
SMEM = pl.BlockSpec(memory_space=pltpu.SMEM)
NEAR = ("y", "core")
PLANES = ("zp", "zq")


def gain_of(scale, residues):
    return residues * jnp.sqrt(scale * (2.0 / SEQ))


def product_kernel(
    near_ref,
    key_hbm,
    value_hbm,
    query_hbm,
    weight_hbm,
    scale_hbm,
    res_hbm,
    out_ref,
    pair_hbm,
    key_ref,
    value_ref,
    query_ref,
    weight_ref,
    scale_ref,
    res_ref,
    prod_ref,
    sems,
):
    loads = [
        pltpu.make_async_copy(src, dst, sems.at[i])
        for i, (src, dst) in enumerate(
            (
                (key_hbm, key_ref),
                (value_hbm, value_ref),
                (query_hbm, query_ref),
                (weight_hbm, weight_ref),
                (scale_hbm, scale_ref),
                (res_hbm, res_ref),
            )
        )
    ]
    for load in loads:
        load.start()
    for load in loads:
        load.wait()
    rows = weight_hbm.shape[0]
    half = pair_hbm.at[pl.ds(pl.multiple_of(near_ref[0] * rows, rows), rows)]
    store = pltpu.make_async_copy(weight_ref, half, sems.at[6])
    store.start()
    tokens = key_ref.shape[0]
    parts, _, lanes = out_ref.shape
    for part in range(parts):
        cols = slice(part * lanes, (part + 1) * lanes)
        product = key_ref[:, cols].astype(F32) * value_ref[:, cols].astype(F32)
        product = product.astype(BF16)
        prod_ref[:, cols] = product.astype(F32)
        out_ref[part, :tokens] = product
        out_ref[part, tokens : 2 * tokens] = query_ref[:, cols]
    scale = scale_ref[...]
    decay = jnp.exp(scale * (-1.0 / SEQ))

    def step(t, state):
        return state * decay + prod_ref[pl.ds(t, 1), :]

    state = lax.fori_loop(0, tokens, step, jnp.zeros(scale.shape, F32), unroll=8)
    state = (state * gain_of(scale, res_ref[...])).astype(BF16)
    for part in range(parts):
        out_ref[part, 2 * tokens :] = state[:, part * lanes : (part + 1) * lanes]
    store.wait()


def states_kernel(slices_ref, scale_ref, totals_ref, after_ref):
    modes, lanes = scale_ref.shape
    parts, rows, _ = slices_ref.shape
    decay = jnp.exp(scale_ref[...] * (-1.0 / 128))
    total = jnp.zeros((modes, lanes), F32)
    for part in range(parts):
        total = total * decay + slices_ref[part, rows - modes :].astype(F32)
    after_ref[...] = total[: after_ref.shape[0]]
    total = total.astype(BF16)
    for copy in range(totals_ref.shape[0]):
        totals_ref[copy] = total


def local_kernel(
    slices_ref, after_ref, scale_ref, res_ref, skip_ref, base_ref, powers_ref, prod_ref
):
    parts, tokens, lanes = prod_ref.shape
    modes = scale_ref.shape[0]
    prod_ref[...] = slices_ref[:, :tokens].astype(F32)
    scale = scale_ref[...]
    decay = jnp.exp(scale * (-1.0 / SEQ))
    gain = gain_of(scale, res_ref[...])
    leap = jnp.exp(scale * (-1.0 / 128))
    starts = [jnp.zeros((modes, lanes), F32)]
    for part in range(parts - 1):
        starts.append(starts[-1] * leap + slices_ref[part, 2 * tokens :].astype(F32))

    def step(t, states):
        fresh = []
        for part, state in enumerate(states):
            state = state * decay + gain * prod_ref[part, pl.ds(t, 1), :]
            base_ref[part, pl.ds(t, 1), :] = jnp.sum(state, axis=0, keepdims=True)
            fresh.append(state)
        return tuple(fresh)

    lax.fori_loop(0, tokens, step, tuple(starts), unroll=4)
    skip = skip_ref[...]
    for part in range(parts):
        base_ref[part] = base_ref[part] + skip * prod_ref[part]
    ages = (lax.broadcasted_iota(jnp.int32, (tokens, lanes), 0) + 1).astype(F32) * (-1.0 / SEQ)
    for mode in range(modes):
        powers_ref[mode] = jnp.exp(ages * scale[mode : mode + 1, :])


def gated_kernel(plane_ref, totals_ref, slices_ref, base_ref, powers_ref, scale_ref, out_ref):
    plane = plane_ref[0]
    parts, tokens, lanes = base_ref.shape
    modes = scale_ref.shape[0]
    scale = scale_ref[...]
    leap = jnp.exp(scale * (-1.0 / 16))
    carry = jnp.zeros(scale.shape, F32)
    for other in range(totals_ref.shape[0]):
        carry = jnp.where(other < plane, carry * leap + totals_ref[other].astype(F32), carry)
    leap = jnp.exp(scale * (-1.0 / 128))
    for part in range(parts):
        conv = base_ref[part]
        for mode in range(modes):
            conv = conv + powers_ref[mode] * carry[mode : mode + 1, :]
        gated = (slices_ref[part, tokens : 2 * tokens].astype(F32) * conv).astype(BF16)
        for row in range(4):
            out_ref[2 * row + part % 2, part // 2] = gated
        carry = carry * leap


def project_kernel(gated_ref, weight_hbm, out_ref, rows_ref, weight_ref, sems):
    parts, blocks, tokens, lanes = gated_ref.shape
    loads = [
        pltpu.make_async_copy(
            weight_hbm.at[256 * quarter : 256 * quarter + 256], weight_ref.at[quarter], sems.at[quarter]
        )
        for quarter in range(4)
    ]
    for load in loads:
        load.start()
    for block in range(blocks):
        for part in range(parts):
            rows_ref[block * tokens : (block + 1) * tokens, part * lanes : (part + 1) * lanes] = (
                gated_ref[part, block]
            )
    order = [4 * far + 2 * core + near for far in range(2) for near in range(2) for core in range(2)]
    for half in range(2):
        quarters = (2 * half, 2 * half + 1)
        for quarter in quarters:
            loads[quarter].wait()
        weight = jnp.concatenate(
            [weight_ref[quarter, 32 * i : 32 * i + 32, :] for quarter in quarters for i in order], axis=0
        )
        terms = lax.dot_general(
            rows_ref[...], weight, (((1,), (1,)), ((), ())), preferred_element_type=F32
        ).astype(BF16)
        for i, quarter in enumerate(quarters):
            for block in range(blocks):
                out_ref[block * 4 + quarter] = terms[
                    block * tokens : (block + 1) * tokens, 256 * i : 256 * i + 256
                ]


def sum_kernel(pieces_ref, out_ref):
    for row in range(4):
        total = pieces_ref[row * 4].astype(F32)
        for owner in range(1, 4):
            total = total + pieces_ref[row * 4 + owner].astype(F32)
        total = total.astype(BF16)
        for plane in range(4):
            start = plane * 256 + row * 64
            out_ref[:, start : start + 64] = total[:, plane * 64 : plane * 64 + 64]


def call(kernel, outs, inputs, specs=None, scratch=(), cost=None, out_spec=None, limit=48):
    single = not isinstance(outs, list)
    return pl.pallas_call(
        kernel,
        out_shape=outs,
        in_specs=specs or [VMEM] * len(inputs),
        out_specs=out_spec or (VMEM if single else [VMEM] * len(outs)),
        scratch_shapes=list(scratch),
        compiler_params=pltpu.CompilerParams(vmem_limit_bytes=int(limit * 1024 * 1024)),
        cost_estimate=cost,
    )(*inputs)


def arr(*shape, dtype=BF16):
    return jax.ShapeDtypeStruct(shape, dtype)


def exchange(pieces, axes):
    return lax.all_to_all(pieces, axes, split_axis=0, concat_axis=0, tiled=True)


def body(query, key, value, scale, residues, skip, out_weight):
    tokens, width = query.shape
    modes = scale.shape[0]
    lanes = width // 8
    z = lax.axis_index(PLANES).astype(jnp.int32)
    load = pltpu.VMEM((tokens, width), BF16)
    near = z.reshape(1) % 2
    slices, half = call(
        product_kernel,
        [arr(8, 2 * tokens + modes, lanes), arr(64, width)],
        (near, key, value, query, out_weight, scale, residues),
        specs=[SMEM] + [HBM] * 6,
        scratch=[
            load,
            load,
            load,
            pltpu.VMEM((32, width), BF16),
            pltpu.VMEM((modes, width), F32),
            pltpu.VMEM((modes, width), F32),
            pltpu.VMEM((tokens, width), F32),
            pltpu.SemaphoreType.DMA((7,)),
        ],
        limit=62,
        cost=pl.CostEstimate(flops=2_000_000, bytes_accessed=4_000_000, transcendentals=0),
    )
    other = lax.ppermute(out_weight, "zq", [(0, 1), (1, 0)])
    pair = lax.dynamic_update_slice_in_dim(half, other, (1 - z % 2) * out_weight.shape[0], 0)
    weight = lax.all_gather(pair, ("zp", "core"), axis=0, tiled=True)
    slices = exchange(slices, NEAR)
    own = lax.axis_index(NEAR) * lanes
    scale, residues, skip = (
        lax.dynamic_slice_in_dim(a, own, lanes, 1) for a in (scale, residues, skip.reshape(1, width))
    )
    work = pltpu.VMEM((8, tokens, lanes), F32)
    totals, after = call(
        states_kernel,
        [arr(16, modes, lanes), arr(8, lanes, dtype=F32)],
        (slices, scale),
    )
    totals = exchange(totals, PLANES)
    base, powers = call(
        local_kernel,
        [arr(8, tokens, lanes, dtype=F32), arr(modes, tokens, lanes, dtype=F32)],
        (slices, after, scale, residues, skip),
        scratch=[work],
        cost=pl.CostEstimate(flops=20_000_000, bytes_accessed=2_000_000, transcendentals=300_000),
    )
    gated = call(
        gated_kernel,
        arr(8, 4, tokens, lanes),
        (z.reshape(1), totals, slices, base, powers, scale),
        specs=[SMEM] + [VMEM] * 5,
    )
    gated = exchange(gated, NEAR)
    terms = call(
        project_kernel,
        arr(16, tokens, 256),
        (gated, weight),
        specs=[VMEM, HBM],
        scratch=[
            pltpu.VMEM((4 * tokens, width), BF16),
            pltpu.VMEM((4, 256, width), BF16),
            pltpu.SemaphoreType.DMA((4,)),
        ],
        limit=50.5,
    )
    terms = exchange(terms, ("y", "x"))
    return call(sum_kernel, arr(tokens, width), (terms,))


def solution(mesh):
    fine = Mesh(mesh.devices.reshape(8, 2, 4, 2, 4), ("zp", "zq", "y", "core", "x"))
    both = P(("zp", "zq", "y", "core"), "x")
    placed = (both, both, both, P(None, "x"), P(None, "x"), P("x"), both)
    return jax.shard_map(body, mesh=fine, in_specs=placed, out_specs=both, check_vma=False)
```

```python
import jax
import jax.numpy as jnp
from jax import lax
from jax.experimental import pallas as pl
from jax.experimental.pallas import tpu as pltpu
from jax.sharding import Mesh
from jax.sharding import PartitionSpec as P

SEQ = 16384
F32 = jnp.float32
BF16 = jnp.bfloat16
VMEM = pl.BlockSpec(memory_space=pltpu.VMEM)
HBM = pl.BlockSpec(memory_space=pltpu.HBM)
SMEM = pl.BlockSpec(memory_space=pltpu.SMEM)
NEAR = ("core", "y")
PLANES = ("zp", "zq")


def member(part):
    return 4 * (part % 2) + part // 2


def gain_of(scale, residues):
    return residues * jnp.sqrt(scale * (2.0 / SEQ))


def product_kernel(
    near_ref,
    key_hbm,
    value_hbm,
    query_hbm,
    weight_hbm,
    out_ref,
    pair_hbm,
    key_ref,
    value_ref,
    query_ref,
    weight_ref,
    sems,
):
    loads = [
        pltpu.make_async_copy(src, dst, sems.at[i])
        for i, (src, dst) in enumerate(
            ((key_hbm, key_ref), (value_hbm, value_ref), (query_hbm, query_ref), (weight_hbm, weight_ref))
        )
    ]
    for load in loads:
        load.start()
    for load in loads:
        load.wait()
    rows = weight_hbm.shape[0]
    half = pair_hbm.at[pl.ds(pl.multiple_of(near_ref[0] * rows, rows), rows)]
    store = pltpu.make_async_copy(weight_ref, half, sems.at[4])
    store.start()
    tokens = key_ref.shape[0]
    parts, _, lanes = out_ref.shape
    for part in range(parts):
        cols = slice(part * lanes, (part + 1) * lanes)
        product = key_ref[:, cols].astype(F32) * value_ref[:, cols].astype(F32)
        out_ref[part, :tokens] = product.astype(BF16)
        out_ref[part, tokens:] = query_ref[:, cols]
    store.wait()


def states_kernel(slices_ref, scale_ref, res_ref, totals_ref, states_ref, prod_ref):
    parts, tokens, lanes = prod_ref.shape
    modes = scale_ref.shape[0]
    for part in range(parts):
        prod_ref[part] = slices_ref[member(part), :tokens].astype(F32)
    scale = scale_ref[...]
    decay = jnp.exp(scale * (-1.0 / SEQ))
    gain = gain_of(scale, res_ref[...])

    def step(t, states):
        return tuple(
            state * decay + prod_ref[part, pl.ds(t, 1), :] for part, state in enumerate(states)
        )

    zero = jnp.zeros((modes, lanes), F32)
    states = lax.fori_loop(0, tokens, step, (zero,) * parts, unroll=8)
    decay = jnp.exp(scale * (-1.0 / 128))
    total = zero
    for part in range(parts):
        state = states[part] * gain
        states_ref[part] = state
        total = total * decay + state
    total = total.astype(BF16)
    for copy in range(totals_ref.shape[0]):
        totals_ref[copy] = total


def local_kernel(
    slices_ref, states_ref, scale_ref, res_ref, skip_ref, base_ref, powers_ref, prod_ref
):
    parts, tokens, lanes = prod_ref.shape
    modes = scale_ref.shape[0]
    for part in range(parts):
        prod_ref[part] = slices_ref[member(part), :tokens].astype(F32)
    scale = scale_ref[...]
    decay = jnp.exp(scale * (-1.0 / SEQ))
    gain = gain_of(scale, res_ref[...])
    leap = jnp.exp(scale * (-1.0 / 128))
    starts = [jnp.zeros((modes, lanes), F32)]
    for part in range(parts - 1):
        starts.append(starts[-1] * leap + states_ref[part])

    def step(t, states):
        fresh = []
        for part, state in enumerate(states):
            state = state * decay + gain * prod_ref[part, pl.ds(t, 1), :]
            base_ref[part, pl.ds(t, 1), :] = jnp.sum(state, axis=0, keepdims=True)
            fresh.append(state)
        return tuple(fresh)

    lax.fori_loop(0, tokens, step, tuple(starts), unroll=4)
    skip = skip_ref[...]
    for part in range(parts):
        base_ref[part] = base_ref[part] + skip * prod_ref[part]
    ages = (lax.broadcasted_iota(jnp.int32, (tokens, lanes), 0) + 1).astype(F32) * (-1.0 / SEQ)
    for mode in range(modes):
        powers_ref[mode] = jnp.exp(ages * scale[mode : mode + 1, :])


def gated_kernel(plane_ref, totals_ref, slices_ref, base_ref, powers_ref, scale_ref, out_ref):
    plane = plane_ref[0]
    parts, tokens, lanes = base_ref.shape
    modes = scale_ref.shape[0]
    scale = scale_ref[...]
    leap = jnp.exp(scale * (-1.0 / 16))
    carry = jnp.zeros(scale.shape, F32)
    for other in range(totals_ref.shape[0]):
        carry = jnp.where(other < plane, carry * leap + totals_ref[other].astype(F32), carry)
    leap = jnp.exp(scale * (-1.0 / 128))
    for part in range(parts):
        conv = base_ref[part]
        for mode in range(modes):
            conv = conv + powers_ref[mode] * carry[mode : mode + 1, :]
        gated = (slices_ref[member(part), tokens:].astype(F32) * conv).astype(BF16)
        for row in range(4):
            out_ref[4 * (part % 2) + row, part // 2] = gated
        carry = carry * leap


def project_kernel(gated_ref, weight_hbm, out_ref, rows_ref, weight_ref, sems):
    parts, blocks, tokens, lanes = gated_ref.shape
    loads = [
        pltpu.make_async_copy(
            weight_hbm.at[256 * quarter : 256 * quarter + 256], weight_ref.at[quarter], sems.at[quarter]
        )
        for quarter in range(4)
    ]
    for load in loads:
        load.start()
    for block in range(blocks):
        for part in range(parts):
            rows_ref[block * tokens : (block + 1) * tokens, part * lanes : (part + 1) * lanes] = (
                gated_ref[part, block]
            )
    order = [4 * far + 2 * core + near for far in range(2) for near in range(2) for core in range(2)]
    for half in range(2):
        quarters = (2 * half, 2 * half + 1)
        for quarter in quarters:
            loads[quarter].wait()
        weight = jnp.concatenate(
            [weight_ref[quarter, 32 * i : 32 * i + 32, :] for quarter in quarters for i in order], axis=0
        )
        terms = lax.dot_general(
            rows_ref[...], weight, (((1,), (1,)), ((), ())), preferred_element_type=F32
        ).astype(BF16)
        for i, quarter in enumerate(quarters):
            for block in range(blocks):
                out_ref[block * 4 + quarter] = terms[
                    block * tokens : (block + 1) * tokens, 256 * i : 256 * i + 256
                ]


def sum_kernel(pieces_ref, out_ref):
    for row in range(4):
        total = pieces_ref[row * 4].astype(F32)
        for owner in range(1, 4):
            total = total + pieces_ref[row * 4 + owner].astype(F32)
        total = total.astype(BF16)
        for plane in range(4):
            start = plane * 256 + row * 64
            out_ref[:, start : start + 64] = total[:, plane * 64 : plane * 64 + 64]


def call(kernel, outs, inputs, specs=None, scratch=(), cost=None, out_spec=None, limit=48):
    single = not isinstance(outs, list)
    return pl.pallas_call(
        kernel,
        out_shape=outs,
        in_specs=specs or [VMEM] * len(inputs),
        out_specs=out_spec or (VMEM if single else [VMEM] * len(outs)),
        scratch_shapes=list(scratch),
        compiler_params=pltpu.CompilerParams(vmem_limit_bytes=int(limit * 1024 * 1024)),
        cost_estimate=cost,
    )(*inputs)


def arr(*shape, dtype=BF16):
    return jax.ShapeDtypeStruct(shape, dtype)


def exchange(pieces, axes):
    return lax.all_to_all(pieces, axes, split_axis=0, concat_axis=0, tiled=True)


def body(query, key, value, scale, residues, skip, out_weight):
    tokens, width = query.shape
    modes = scale.shape[0]
    lanes = width // 8
    z = lax.axis_index(PLANES).astype(jnp.int32)
    load = pltpu.VMEM((tokens, width), BF16)
    near = z.reshape(1) % 2
    slices, half = call(
        product_kernel,
        [arr(8, 2 * tokens, lanes), arr(64, width)],
        (near, key, value, query, out_weight),
        specs=[SMEM] + [HBM] * 4,
        scratch=[load, load, load, pltpu.VMEM((32, width), BF16), pltpu.SemaphoreType.DMA((5,))],
        limit=62,
        cost=pl.CostEstimate(flops=2_000_000, bytes_accessed=4_000_000, transcendentals=0),
    )
    other = lax.ppermute(out_weight, "zq", [(0, 1), (1, 0)])
    pair = lax.dynamic_update_slice_in_dim(half, other, (1 - z % 2) * out_weight.shape[0], 0)
    weight = lax.all_gather(pair, ("zp", "core"), axis=0, tiled=True)
    slices = exchange(slices, NEAR)
    own = lax.axis_index(NEAR) * lanes
    scale, residues, skip = (
        lax.dynamic_slice_in_dim(a, own, lanes, 1) for a in (scale, residues, skip.reshape(1, width))
    )
    work = pltpu.VMEM((8, tokens, lanes), F32)
    totals, states = call(
        states_kernel,
        [arr(16, modes, lanes), arr(8, modes, lanes, dtype=F32)],
        (slices, scale, residues),
        scratch=[work],
        cost=pl.CostEstimate(flops=20_000_000, bytes_accessed=2_000_000, transcendentals=0),
    )
    totals = exchange(totals, PLANES)
    base, powers = call(
        local_kernel,
        [arr(8, tokens, lanes, dtype=F32), arr(modes, tokens, lanes, dtype=F32)],
        (slices, states, scale, residues, skip),
        scratch=[work],
        cost=pl.CostEstimate(flops=20_000_000, bytes_accessed=2_000_000, transcendentals=300_000),
    )
    gated = call(
        gated_kernel,
        arr(8, 4, tokens, lanes),
        (z.reshape(1), totals, slices, base, powers, scale),
        specs=[SMEM] + [VMEM] * 5,
    )
    gated = exchange(gated, NEAR)
    terms = call(
        project_kernel,
        arr(16, tokens, 256),
        (gated, weight),
        specs=[VMEM, HBM],
        scratch=[
            pltpu.VMEM((4 * tokens, width), BF16),
            pltpu.VMEM((4, 256, width), BF16),
            pltpu.SemaphoreType.DMA((4,)),
        ],
        limit=50.5,
    )
    terms = exchange(terms, ("y", "x"))
    return call(sum_kernel, arr(tokens, width), (terms,))


def solution(mesh):
    fine = Mesh(mesh.devices.reshape(8, 2, 4, 2, 4), ("zp", "zq", "y", "core", "x"))
    both = P(("zp", "zq", "y", "core"), "x")
    placed = (both, both, both, P(None, "x"), P(None, "x"), P("x"), both)
    return jax.shard_map(body, mesh=fine, in_specs=placed, out_specs=both, check_vma=False)
```

```python
import jax
import jax.numpy as jnp
from jax import lax
from jax.experimental import pallas as pl
from jax.experimental.pallas import tpu as pltpu
from jax.sharding import Mesh
from jax.sharding import PartitionSpec as P

SEQ = 16384
F32 = jnp.float32
BF16 = jnp.bfloat16
VMEM = pl.BlockSpec(memory_space=pltpu.VMEM)
HBM = pl.BlockSpec(memory_space=pltpu.HBM)
SMEM = pl.BlockSpec(memory_space=pltpu.SMEM)
NEAR = ("core", "y")
PLANES = ("zp", "zq")


def member(part):
    return 4 * (part % 2) + part // 2


def gain_of(scale, residues):
    return residues * jnp.sqrt(scale * (2.0 / SEQ))


def product_kernel(
    near_ref,
    key_hbm,
    value_hbm,
    query_hbm,
    weight_hbm,
    out_ref,
    pair_hbm,
    key_ref,
    value_ref,
    query_ref,
    weight_ref,
    sems,
):
    loads = [
        pltpu.make_async_copy(src, dst, sems.at[i])
        for i, (src, dst) in enumerate(
            ((key_hbm, key_ref), (value_hbm, value_ref), (query_hbm, query_ref), (weight_hbm, weight_ref))
        )
    ]
    for load in loads:
        load.start()
    for load in loads:
        load.wait()
    rows = weight_hbm.shape[0]
    half = pair_hbm.at[pl.ds(pl.multiple_of(near_ref[0] * rows, rows), rows)]
    store = pltpu.make_async_copy(weight_ref, half, sems.at[4])
    store.start()
    tokens = key_ref.shape[0]
    parts, _, lanes = out_ref.shape
    for part in range(parts):
        cols = slice(part * lanes, (part + 1) * lanes)
        product = key_ref[:, cols].astype(F32) * value_ref[:, cols].astype(F32)
        out_ref[part, :tokens] = product.astype(BF16)
        out_ref[part, tokens:] = query_ref[:, cols]
    store.wait()


def states_kernel(slices_ref, scale_ref, res_ref, totals_ref, states_ref, prod_ref):
    parts, tokens, lanes = prod_ref.shape
    modes = scale_ref.shape[0]
    for part in range(parts):
        prod_ref[part] = slices_ref[member(part), :tokens].astype(F32)
    scale = scale_ref[...]
    decay = jnp.exp(scale * (-1.0 / SEQ))
    gain = gain_of(scale, res_ref[...])

    def step(t, states):
        return tuple(
            state * decay + prod_ref[part, pl.ds(t, 1), :] for part, state in enumerate(states)
        )

    zero = jnp.zeros((modes, lanes), F32)
    states = lax.fori_loop(0, tokens, step, (zero,) * parts, unroll=8)
    decay = jnp.exp(scale * (-1.0 / 128))
    total = zero
    for part in range(parts):
        state = states[part] * gain
        states_ref[part] = state
        total = total * decay + state
    total = total.astype(BF16)
    for copy in range(totals_ref.shape[0]):
        totals_ref[copy] = total


def local_kernel(
    slices_ref, states_ref, scale_ref, res_ref, skip_ref, base_ref, powers_ref, prod_ref
):
    parts, tokens, lanes = prod_ref.shape
    modes = scale_ref.shape[0]
    for part in range(parts):
        prod_ref[part] = slices_ref[member(part), :tokens].astype(F32)
    scale = scale_ref[...]
    decay = jnp.exp(scale * (-1.0 / SEQ))
    gain = gain_of(scale, res_ref[...])
    leap = jnp.exp(scale * (-1.0 / 128))
    starts = [jnp.zeros((modes, lanes), F32)]
    for part in range(parts - 1):
        starts.append(starts[-1] * leap + states_ref[part])

    def step(t, states):
        fresh = []
        for part, state in enumerate(states):
            state = state * decay + gain * prod_ref[part, pl.ds(t, 1), :]
            base_ref[part, pl.ds(t, 1), :] = jnp.sum(state, axis=0, keepdims=True)
            fresh.append(state)
        return tuple(fresh)

    lax.fori_loop(0, tokens, step, tuple(starts), unroll=4)
    skip = skip_ref[...]
    for part in range(parts):
        base_ref[part] = base_ref[part] + skip * prod_ref[part]
    ages = (lax.broadcasted_iota(jnp.int32, (tokens, lanes), 0) + 1).astype(F32) * (-1.0 / SEQ)
    for mode in range(modes):
        powers_ref[mode] = jnp.exp(ages * scale[mode : mode + 1, :])


def gated_kernel(plane_ref, totals_ref, slices_ref, base_ref, powers_ref, scale_ref, out_ref):
    plane = plane_ref[0]
    parts, tokens, lanes = base_ref.shape
    modes = scale_ref.shape[0]
    scale = scale_ref[...]
    leap = jnp.exp(scale * (-1.0 / 16))
    carry = jnp.zeros(scale.shape, F32)
    for other in range(totals_ref.shape[0]):
        carry = jnp.where(other < plane, carry * leap + totals_ref[other].astype(F32), carry)
    leap = jnp.exp(scale * (-1.0 / 128))
    for part in range(parts):
        conv = base_ref[part]
        for mode in range(modes):
            conv = conv + powers_ref[mode] * carry[mode : mode + 1, :]
        gated = (slices_ref[member(part), tokens:].astype(F32) * conv).astype(BF16)
        for row in range(4):
            out_ref[4 * (part % 2) + row, part // 2] = gated
        carry = carry * leap


def project_kernel(gated_ref, weight_hbm, out_ref, rows_ref, weight_ref, sems):
    parts, blocks, tokens, lanes = gated_ref.shape
    loads = [
        pltpu.make_async_copy(
            weight_hbm.at[256 * quarter : 256 * quarter + 256], weight_ref.at[quarter], sems.at[quarter]
        )
        for quarter in range(4)
    ]
    for load in loads:
        load.start()
    for block in range(blocks):
        for part in range(parts):
            rows_ref[block * tokens : (block + 1) * tokens, part * lanes : (part + 1) * lanes] = (
                gated_ref[part, block]
            )
    order = [4 * far + 2 * core + near for far in range(2) for near in range(2) for core in range(2)]
    for half in range(2):
        quarters = (2 * half, 2 * half + 1)
        for quarter in quarters:
            loads[quarter].wait()
        weight = jnp.concatenate(
            [weight_ref[quarter, 32 * i : 32 * i + 32, :] for quarter in quarters for i in order], axis=0
        )
        terms = lax.dot_general(
            rows_ref[...], weight, (((1,), (1,)), ((), ())), preferred_element_type=F32
        ).astype(BF16)
        for i, quarter in enumerate(quarters):
            for block in range(blocks):
                out_ref[quarter * 4 + block] = terms[
                    block * tokens : (block + 1) * tokens, 256 * i : 256 * i + 256
                ]


def sum_kernel(pieces_ref, out_ref):
    for row in range(4):
        total = pieces_ref[row].astype(F32)
        for owner in range(1, 4):
            total = total + pieces_ref[owner * 4 + row].astype(F32)
        total = total.astype(BF16)
        for plane in range(4):
            start = plane * 256 + row * 64
            out_ref[:, start : start + 64] = total[:, plane * 64 : plane * 64 + 64]


def call(kernel, outs, inputs, specs=None, scratch=(), cost=None, out_spec=None, limit=48):
    single = not isinstance(outs, list)
    return pl.pallas_call(
        kernel,
        out_shape=outs,
        in_specs=specs or [VMEM] * len(inputs),
        out_specs=out_spec or (VMEM if single else [VMEM] * len(outs)),
        scratch_shapes=list(scratch),
        compiler_params=pltpu.CompilerParams(vmem_limit_bytes=int(limit * 1024 * 1024)),
        cost_estimate=cost,
    )(*inputs)


def arr(*shape, dtype=BF16):
    return jax.ShapeDtypeStruct(shape, dtype)


def exchange(pieces, axes):
    return lax.all_to_all(pieces, axes, split_axis=0, concat_axis=0, tiled=True)


def body(query, key, value, scale, residues, skip, out_weight):
    tokens, width = query.shape
    modes = scale.shape[0]
    lanes = width // 8
    z = lax.axis_index(PLANES).astype(jnp.int32)
    load = pltpu.VMEM((tokens, width), BF16)
    near = z.reshape(1) % 2
    slices, half = call(
        product_kernel,
        [arr(8, 2 * tokens, lanes), arr(64, width)],
        (near, key, value, query, out_weight),
        specs=[SMEM] + [HBM] * 4,
        scratch=[load, load, load, pltpu.VMEM((32, width), BF16), pltpu.SemaphoreType.DMA((5,))],
        limit=62,
        cost=pl.CostEstimate(flops=2_000_000, bytes_accessed=4_000_000, transcendentals=0),
    )
    other = lax.ppermute(out_weight, "zq", [(0, 1), (1, 0)])
    pair = lax.dynamic_update_slice_in_dim(half, other, (1 - z % 2) * out_weight.shape[0], 0)
    weight = lax.all_gather(pair, ("zp", "core"), axis=0, tiled=True)
    slices = exchange(slices, NEAR)
    own = lax.axis_index(NEAR) * lanes
    scale, residues, skip = (
        lax.dynamic_slice_in_dim(a, own, lanes, 1) for a in (scale, residues, skip.reshape(1, width))
    )
    work = pltpu.VMEM((8, tokens, lanes), F32)
    totals, states = call(
        states_kernel,
        [arr(16, modes, lanes), arr(8, modes, lanes, dtype=F32)],
        (slices, scale, residues),
        scratch=[work],
        cost=pl.CostEstimate(flops=20_000_000, bytes_accessed=2_000_000, transcendentals=0),
    )
    totals = exchange(totals, PLANES)
    base, powers = call(
        local_kernel,
        [arr(8, tokens, lanes, dtype=F32), arr(modes, tokens, lanes, dtype=F32)],
        (slices, states, scale, residues, skip),
        scratch=[work],
        cost=pl.CostEstimate(flops=20_000_000, bytes_accessed=2_000_000, transcendentals=300_000),
    )
    gated = call(
        gated_kernel,
        arr(8, 4, tokens, lanes),
        (z.reshape(1), totals, slices, base, powers, scale),
        specs=[SMEM] + [VMEM] * 5,
    )
    gated = exchange(gated, NEAR)
    terms = call(
        project_kernel,
        arr(16, tokens, 256),
        (gated, weight),
        specs=[VMEM, HBM],
        scratch=[
            pltpu.VMEM((4 * tokens, width), BF16),
            pltpu.VMEM((4, 256, width), BF16),
            pltpu.SemaphoreType.DMA((4,)),
        ],
        limit=50.5,
    )
    terms = exchange(terms, ("x", "y"))
    return call(sum_kernel, arr(tokens, width), (terms,))


def solution(mesh):
    fine = Mesh(mesh.devices.reshape(8, 2, 4, 2, 4), ("zp", "zq", "y", "core", "x"))
    both = P(("zp", "zq", "y", "core"), "x")
    placed = (both, both, both, P(None, "x"), P(None, "x"), P("x"), both)
    return jax.shard_map(body, mesh=fine, in_specs=placed, out_specs=both, check_vma=False)
```

```python
import jax
import jax.numpy as jnp
from jax import lax
from jax.experimental import pallas as pl
from jax.experimental.pallas import tpu as pltpu
from jax.sharding import Mesh
from jax.sharding import PartitionSpec as P

SEQ = 16384
F32 = jnp.float32
BF16 = jnp.bfloat16
VMEM = pl.BlockSpec(memory_space=pltpu.VMEM)
HBM = pl.BlockSpec(memory_space=pltpu.HBM)
SMEM = pl.BlockSpec(memory_space=pltpu.SMEM)
NEAR = ("core", "y")
PLANES = ("zp", "zq")


def member(part):
    return 4 * (part % 2) + part // 2


def gain_of(scale, residues):
    return residues * jnp.sqrt(scale * (2.0 / SEQ))


def product_kernel(
    near_ref,
    key_hbm,
    value_hbm,
    query_hbm,
    weight_hbm,
    out_ref,
    pair_hbm,
    key_ref,
    value_ref,
    query_ref,
    weight_ref,
    sems,
):
    loads = [
        pltpu.make_async_copy(src, dst, sems.at[i])
        for i, (src, dst) in enumerate(
            ((key_hbm, key_ref), (value_hbm, value_ref), (query_hbm, query_ref), (weight_hbm, weight_ref))
        )
    ]
    for load in loads:
        load.start()
    for load in loads:
        load.wait()
    rows = weight_hbm.shape[0]
    half = pair_hbm.at[pl.ds(pl.multiple_of(near_ref[0] * rows, rows), rows)]
    store = pltpu.make_async_copy(weight_ref, half, sems.at[4])
    store.start()
    tokens = key_ref.shape[0]
    parts, _, lanes = out_ref.shape
    for part in range(parts):
        cols = slice(part * lanes, (part + 1) * lanes)
        product = key_ref[:, cols].astype(F32) * value_ref[:, cols].astype(F32)
        out_ref[part, :tokens] = product.astype(BF16)
        out_ref[part, tokens:] = query_ref[:, cols]
    store.wait()


def states_kernel(slices_ref, scale_ref, res_ref, totals_ref, states_ref, prod_ref):
    parts, tokens, lanes = prod_ref.shape
    modes = scale_ref.shape[0]
    for part in range(parts):
        prod_ref[part] = slices_ref[member(part), :tokens].astype(F32)
    scale = scale_ref[...]
    decay = jnp.exp(scale * (-1.0 / SEQ))
    gain = gain_of(scale, res_ref[...])

    def step(t, states):
        return tuple(
            state * decay + prod_ref[part, pl.ds(t, 1), :] for part, state in enumerate(states)
        )

    zero = jnp.zeros((modes, lanes), F32)
    states = lax.fori_loop(0, tokens, step, (zero,) * parts, unroll=16)
    decay = jnp.exp(scale * (-1.0 / 128))
    total = zero
    for part in range(parts):
        state = states[part] * gain
        states_ref[part] = state
        total = total * decay + state
    total = total.astype(BF16)
    for copy in range(totals_ref.shape[0]):
        totals_ref[copy] = total


def local_kernel(
    slices_ref, states_ref, scale_ref, res_ref, skip_ref, base_ref, powers_ref, prod_ref
):
    parts, tokens, lanes = prod_ref.shape
    modes = scale_ref.shape[0]
    for part in range(parts):
        prod_ref[part] = slices_ref[member(part), :tokens].astype(F32)
    scale = scale_ref[...]
    decay = jnp.exp(scale * (-1.0 / SEQ))
    gain = gain_of(scale, res_ref[...])
    leap = jnp.exp(scale * (-1.0 / 128))
    starts = [jnp.zeros((modes, lanes), F32)]
    for part in range(parts - 1):
        starts.append(starts[-1] * leap + states_ref[part])

    def step(t, states):
        fresh = []
        for part, state in enumerate(states):
            state = state * decay + gain * prod_ref[part, pl.ds(t, 1), :]
            base_ref[part, pl.ds(t, 1), :] = jnp.sum(state, axis=0, keepdims=True)
            fresh.append(state)
        return tuple(fresh)

    lax.fori_loop(0, tokens, step, tuple(starts), unroll=4)
    skip = skip_ref[...]
    for part in range(parts):
        base_ref[part] = base_ref[part] + skip * prod_ref[part]
    ages = (lax.broadcasted_iota(jnp.int32, (tokens, lanes), 0) + 1).astype(F32) * (-1.0 / SEQ)
    for mode in range(modes):
        powers_ref[mode] = jnp.exp(ages * scale[mode : mode + 1, :])


def gated_kernel(plane_ref, totals_ref, slices_ref, base_ref, powers_ref, scale_ref, out_ref):
    plane = plane_ref[0]
    parts, tokens, lanes = base_ref.shape
    modes = scale_ref.shape[0]
    scale = scale_ref[...]
    leap = jnp.exp(scale * (-1.0 / 16))
    carry = jnp.zeros(scale.shape, F32)
    for other in range(totals_ref.shape[0]):
        carry = jnp.where(other < plane, carry * leap + totals_ref[other].astype(F32), carry)
    leap = jnp.exp(scale * (-1.0 / 128))
    for part in range(parts):
        conv = base_ref[part]
        for mode in range(modes):
            conv = conv + powers_ref[mode] * carry[mode : mode + 1, :]
        gated = (slices_ref[member(part), tokens:].astype(F32) * conv).astype(BF16)
        for row in range(4):
            out_ref[4 * (part % 2) + row, part // 2] = gated
        carry = carry * leap


def project_kernel(gated_ref, weight_hbm, out_ref, rows_ref, weight_ref, sems):
    parts, blocks, tokens, lanes = gated_ref.shape
    loads = [
        pltpu.make_async_copy(
            weight_hbm.at[256 * quarter : 256 * quarter + 256], weight_ref.at[quarter], sems.at[quarter]
        )
        for quarter in range(4)
    ]
    for load in loads:
        load.start()
    for block in range(blocks):
        for part in range(parts):
            rows_ref[block * tokens : (block + 1) * tokens, part * lanes : (part + 1) * lanes] = (
                gated_ref[part, block]
            )
    order = [4 * far + 2 * core + near for far in range(2) for near in range(2) for core in range(2)]
    for half in range(2):
        quarters = (2 * half, 2 * half + 1)
        for quarter in quarters:
            loads[quarter].wait()
        weight = jnp.concatenate(
            [weight_ref[quarter, 32 * i : 32 * i + 32, :] for quarter in quarters for i in order], axis=0
        )
        terms = lax.dot_general(
            rows_ref[...], weight, (((1,), (1,)), ((), ())), preferred_element_type=F32
        ).astype(BF16)
        for i, quarter in enumerate(quarters):
            for block in range(blocks):
                out_ref[block * 4 + quarter] = terms[
                    block * tokens : (block + 1) * tokens, 256 * i : 256 * i + 256
                ]


def sum_kernel(pieces_ref, out_ref):
    for row in range(4):
        total = pieces_ref[row * 4].astype(F32)
        for owner in range(1, 4):
            total = total + pieces_ref[row * 4 + owner].astype(F32)
        total = total.astype(BF16)
        for plane in range(4):
            start = plane * 256 + row * 64
            out_ref[:, start : start + 64] = total[:, plane * 64 : plane * 64 + 64]


def call(kernel, outs, inputs, specs=None, scratch=(), cost=None, out_spec=None, limit=48):
    single = not isinstance(outs, list)
    return pl.pallas_call(
        kernel,
        out_shape=outs,
        in_specs=specs or [VMEM] * len(inputs),
        out_specs=out_spec or (VMEM if single else [VMEM] * len(outs)),
        scratch_shapes=list(scratch),
        compiler_params=pltpu.CompilerParams(vmem_limit_bytes=int(limit * 1024 * 1024)),
        cost_estimate=cost,
    )(*inputs)


def arr(*shape, dtype=BF16):
    return jax.ShapeDtypeStruct(shape, dtype)


def exchange(pieces, axes):
    return lax.all_to_all(pieces, axes, split_axis=0, concat_axis=0, tiled=True)


def body(query, key, value, scale, residues, skip, out_weight):
    tokens, width = query.shape
    modes = scale.shape[0]
    lanes = width // 8
    z = lax.axis_index(PLANES).astype(jnp.int32)
    load = pltpu.VMEM((tokens, width), BF16)
    near = z.reshape(1) % 2
    slices, half = call(
        product_kernel,
        [arr(8, 2 * tokens, lanes), arr(64, width)],
        (near, key, value, query, out_weight),
        specs=[SMEM] + [HBM] * 4,
        scratch=[load, load, load, pltpu.VMEM((32, width), BF16), pltpu.SemaphoreType.DMA((5,))],
        limit=62,
        cost=pl.CostEstimate(flops=2_000_000, bytes_accessed=4_000_000, transcendentals=0),
    )
    other = lax.ppermute(out_weight, "zq", [(0, 1), (1, 0)])
    pair = lax.dynamic_update_slice_in_dim(half, other, (1 - z % 2) * out_weight.shape[0], 0)
    weight = lax.all_gather(pair, ("zp", "core"), axis=0, tiled=True)
    slices = exchange(slices, NEAR)
    own = lax.axis_index(NEAR) * lanes
    scale, residues, skip = (
        lax.dynamic_slice_in_dim(a, own, lanes, 1) for a in (scale, residues, skip.reshape(1, width))
    )
    work = pltpu.VMEM((8, tokens, lanes), F32)
    totals, states = call(
        states_kernel,
        [arr(16, modes, lanes), arr(8, modes, lanes, dtype=F32)],
        (slices, scale, residues),
        scratch=[work],
        cost=pl.CostEstimate(flops=20_000_000, bytes_accessed=2_000_000, transcendentals=0),
    )
    totals = exchange(totals, PLANES)
    base, powers = call(
        local_kernel,
        [arr(8, tokens, lanes, dtype=F32), arr(modes, tokens, lanes, dtype=F32)],
        (slices, states, scale, residues, skip),
        scratch=[work],
        cost=pl.CostEstimate(flops=20_000_000, bytes_accessed=2_000_000, transcendentals=300_000),
    )
    gated = call(
        gated_kernel,
        arr(8, 4, tokens, lanes),
        (z.reshape(1), totals, slices, base, powers, scale),
        specs=[SMEM] + [VMEM] * 5,
    )
    gated = exchange(gated, NEAR)
    terms = call(
        project_kernel,
        arr(16, tokens, 256),
        (gated, weight),
        specs=[VMEM, HBM],
        scratch=[
            pltpu.VMEM((4 * tokens, width), BF16),
            pltpu.VMEM((4, 256, width), BF16),
            pltpu.SemaphoreType.DMA((4,)),
        ],
        limit=50.5,
    )
    terms = exchange(terms, ("y", "x"))
    return call(sum_kernel, arr(tokens, width), (terms,))


def solution(mesh):
    fine = Mesh(mesh.devices.reshape(8, 2, 4, 2, 4), ("zp", "zq", "y", "core", "x"))
    both = P(("zp", "zq", "y", "core"), "x")
    placed = (both, both, both, P(None, "x"), P(None, "x"), P("x"), both)
    return jax.shard_map(body, mesh=fine, in_specs=placed, out_specs=both, check_vma=False)
```
